512 devices in a mesh: gx: 8 (over z_hi, x), gy: 32 (over z_lo, y), gz: 2 (over core).
Axes of the slice: x: 4, y: 4, z: 16 (z_hi: 2, z_lo: 8; z = z_hi * 8 + z_lo), core: 2. Of those that a mesh axis runs over, the one named last changes fastest.
Arguments:
- fields: float32 [2, 16, 2048, 2048], P(None, 'gz', 'gy', 'gx'), may hold values from -6 to 6
- factor: float32 [2048, 128], replicated, may hold values from -0.125 to 0.125
Outputs:
- gram: float32 [2048, 2048], P('gy', ('gx', 'gz'))
The draws below stay inside these ranges and needn't reach their ends.
All inputs are finite; a program needn't handle non-finite values.
Results may differ from the reference program's by a relative error of at most 0.000054.
Values sent between devices are 32-bit elements; how exact they have to be, the bound alone decides.
A program may use at most 64 MiB of HBM per device.

```python
import jax
import jax.numpy as jnp
from jax import lax

NX = 2048
NY = 2048
RANK = 128
NZ = 16


def shard_levels(rng, dims, pieces, low, largest):
    level, own = 1.0, jax.random.fold_in(rng, 6)
    for position, shards_of in pieces:
        steps = jnp.exp(jax.random.uniform(jax.random.fold_in(own, position), (shards_of,), jnp.float32, low / len(pieces), largest / len(pieces)))
        level = level * jnp.repeat(steps, dims[position] // shards_of).reshape([-1 if axis == position else 1 for axis in range(len(dims))])
    return level


def noise(rng, shape, spread, bound, split=(), kind=jnp.bfloat16):
    array = spread * jax.random.normal(rng, shape, jnp.float32)
    if split:
        array = array * shard_levels(rng, shape, split, -0.22, 0.18)
    return jnp.clip(array, -bound, bound).astype(kind)


def setup_inputs(seed: int = 0) -> dict:
    key_list = jax.random.split(jax.random.key(seed), 3)
    return {
        "fields": noise(key_list[0], (2, NZ, NY, NX), 1.0, 6.0, ((1, 2), (2, 32), (3, 8)), jnp.float32),
        "factor": noise(key_list[1], (NX, RANK), NX ** -0.5, 0.125, (), jnp.float32),
    }


def smooth_along(padded, axis_dim):
    length = padded.shape[axis_dim] - 4

    def shifted(offset):
        return lax.slice_in_dim(padded, offset, offset + length, axis=axis_dim)
    return (shifted(0) + 4.0 * shifted(1) + 6.0 * shifted(2) + 4.0 * shifted(3) + shifted(4)) * 0.0625

def reference(fields, factor):

    def one_plane(zindex):
        plane = lax.dynamic_index_in_dim(fields, zindex, 1, keepdims=False)
        smooth_x = smooth_along(jnp.pad(plane, ((0, 0), (0, 0), (2, 2))), 2)
        smoothed = smooth_along(jnp.pad(smooth_x, ((0, 0), (2, 2), (0, 0))), 1)
        return jnp.einsum('vyx,xr->vyr', smoothed, factor, precision=lax.Precision.HIGHEST)
    projected = lax.map(one_plane, jnp.arange(NZ, dtype=jnp.int32))
    gram = jnp.einsum('zvar,zvbr->ab', projected, projected, precision=lax.Precision.HIGHEST)
    return gram * (1.0 / jnp.sqrt(jnp.float32(2 * NZ * RANK)))
```

```python
import jax
import jax.numpy as jnp
from jax import lax
from jax.experimental import pallas as pl
from jax.experimental.pallas import tpu as pltpu
from jax.sharding import PartitionSpec as P

MESH = pl.DeviceIdType.MESH
HIGHEST = lax.Precision.HIGHEST
NT = (((1,), (1,)), ((), ()))

XRS, ZHI, HALO, RZ, CA, RY, CY, GRS, FIN = 0, 3, 4, 8, 11, 12, 16, 18, 25
COPIES = 29


def smooth(p, length):
    return (
        p[0:length] + 4.0 * p[1 : length + 1] + 6.0 * p[2 : length + 2]
        + 4.0 * p[3 : length + 3] + p[4 : length + 4]
    ) * 0.0625


def kernel(
    f_ref, fac_ref, o_ref,
    fac, sf, part, xin, tsum, zin, hin, rbuf, cbuf, gsend, gin, wsend, win,
    fsem, ssem, rsem, lsem,
):
    gx, gy, k = lax.axis_index("gx"), lax.axis_index("gy"), lax.axis_index("gz")
    h, x = gx // 4, gx % 4
    zlo, y = gy // 4, gy % 4
    a, m = zlo // 4, zlo % 4
    ye, yd = y + 1 - 2 * (y % 2), 3 - y

    def dev(h=h, x=x, a=a, m=m, y=y, k=k):
        return (h * 4 + x, (a * 4 + m) * 4 + y, k)

    x_peers = [(x + d) % 4 for d in range(1, 4)]
    m_peers = [(m + d) % 4 for d in range(1, 4)]
    g_peers = [((x + dx) % 4, (k + dk) % 2) for dx in range(4) for dk in range(2) if dx + dk]
    up, down = (gy + 1) % 32, (gy + 31) % 32
    fin_self = x == m

    barrier = pltpu.get_barrier_semaphore()

    def greet(d):
        pl.semaphore_signal(barrier, inc=1, device_id=d, device_id_type=MESH)

    for xp, kp in g_peers:
        greet(dev(x=xp, k=kp))
    for mp in m_peers:
        greet(dev(m=mp))
    greet(dev(h=1 - h))
    greet(dev(a=1 - a))
    greet(dev(y=ye))
    greet(dev(y=yd))
    for rel in range(2):
        hq = (h + rel) % 2
        greet((hq * 4 + x, up, k))
        greet((hq * 4 + x, down, k))
        greet(dev(h=hq, x=m, m=x, y=ye))
    greet(dev(h=1 - h, x=m, m=x))

    @pl.when(jnp.logical_not(fin_self))
    def _():
        greet(dev(x=m, m=x))

    lo = pl.multiple_of(jnp.maximum(gx * 256 - 8, 0), 8)
    mid = pl.multiple_of(gx * 256, 8)
    hi = pl.multiple_of(jnp.minimum(gx * 256 + 256, 2040), 8)
    loads = [
        pltpu.make_async_copy(fac_ref.at[pl.ds(lo, 8)], fac.at[pl.ds(0, 8)], fsem.at[0]),
        pltpu.make_async_copy(fac_ref.at[pl.ds(mid, 256)], fac.at[pl.ds(8, 256)], fsem.at[1]),
        pltpu.make_async_copy(fac_ref.at[pl.ds(hi, 8)], fac.at[pl.ds(264, 8)], fsem.at[2]),
    ]
    for c in loads:
        c.start()
    for c in loads:
        c.wait()
    before = jnp.where(gx > 0, fac[6:8, :], 0.0)
    after = jnp.where(gx < 7, fac[264:266, :], 0.0)
    sf[...] = smooth(jnp.concatenate([before, fac[8:264, :], after], axis=0), 256)

    sends = []

    def send(src, dst, number, device):
        c = pltpu.make_async_remote_copy(
            src_ref=src, dst_ref=dst, send_sem=ssem.at[number], recv_sem=rsem.at[number],
            device_id=device, device_id_type=MESH,
        )
        c.start()
        sends.append(c)
        return c

    def project(xp):
        w = sf[...]
        for v in range(2):
            for q in range(2):
                rows = f_ref[v, 2 * xp + q]
                part[xp, q, v] = jnp.dot(
                    rows, w, precision=HIGHEST, preferred_element_type=jnp.float32
                )

    copies = []
    for i, d in enumerate((2, 1, 3)):
        xp = x_peers[d - 1]
        project(xp)
        if i == 0:
            pl.semaphore_wait(barrier, jnp.where(fin_self, 21, 22))
        copies.append(send(part.at[xp], xin.at[d - 1], XRS + d - 1, dev(x=xp)))
    project(x)
    for c in copies:
        c.wait_recv()
    tsum[...] = part[x] + xin[0] + xin[1] + xin[2]

    copies = [send(tsum.at[1 - h], zin, ZHI, dev(h=1 - h))]
    for rel in (1, 0):
        hq = (h + rel) % 2
        copies.append(
            send(tsum.at[hq, :, pl.ds(0, 8)], hin.at[1, rel], HALO + 2 + rel, (hq * 4 + x, down, k))
        )
        copies.append(
            send(tsum.at[hq, :, pl.ds(56, 8)], hin.at[0, rel], HALO + rel, (hq * 4 + x, up, k))
        )
    for c in copies:
        c.wait_recv()
    for v in range(2):
        before = jnp.where(gy > 0, hin[0, 0, v, 6:8] + hin[0, 1, v, 6:8], 0.0)
        after = jnp.where(gy < 31, hin[1, 0, v, 0:2] + hin[1, 1, v, 0:2], 0.0)
        own = tsum[h, v] + zin[v]
        block = smooth(jnp.concatenate([before, own, after], axis=0), 64)
        rbuf[0, m, :, v * 128 : (v + 1) * 128] = block
        cbuf[a, 0, :, v * 128 : (v + 1) * 128] = block

    mine = rbuf.at[0, m]
    far = send(mine, cbuf.at[a, 0], CA, dev(a=1 - a))
    zs = [send(mine, rbuf.at[0, m], RZ + d, dev(m=m_peers[d])) for d in range(3)]
    copies = [
        send(mine, rbuf.at[1, m], RY, dev(y=ye)),
        send(mine, cbuf.at[a, 1], CY, dev(y=yd)),
    ]
    for d in (0, 2, 1):
        zs[d].wait_recv()
        src = (m + 3 - d) % 4
        copies.append(send(rbuf.at[0, src], rbuf.at[1, src], RY + 1 + d, dev(y=ye)))
    far.wait_recv()
    copies.append(send(cbuf.at[1 - a, 0], cbuf.at[1 - a, 1], CY + 1, dev(y=yd)))
    for c in copies:
        c.wait_recv()

    def tile(mp, kp):
        jd = jnp.where(y // 2 == kp, 0, 1)
        rows = jnp.concatenate([rbuf[0, mp], rbuf[1, mp]], axis=0)
        cols = jnp.concatenate([cbuf[0, jd], cbuf[1, jd]], axis=0)
        return lax.dot_general(
            rows, cols, NT, precision=HIGHEST, preferred_element_type=jnp.float32
        )

    copies = []
    for i in (3, 4, 1, 2, 5, 6, 0):
        xp, kp = g_peers[i]
        gsend[i] = tile(xp, kp)
        copies.append(send(gsend.at[i], gin.at[i], GRS + i, dev(x=xp, k=kp)))
    total = tile(x, k)
    for c in copies:
        c.wait_recv()
    for i in range(7):
        total = total + gin[i]

    copies = []
    for rel in (1, 0):
        aq = (h + rel) % 2
        cols = jnp.where(aq == 0, total[:, 0:64], total[:, 64:128])
        for j in (1, 0):
            u = cols[j * 64 : (j + 1) * 64]
            wsend[rel, j] = jnp.concatenate([u[0:32], u[32:64]], axis=1)
            target = dev(h=aq, x=m, m=x, y=ye if j else y)
            number = FIN + 2 * rel + j
            if rel or j:
                copies.append(send(wsend.at[rel, j], win.at[rel, j], number, target))
            else:
                own = pltpu.make_async_copy(wsend.at[0, 0], win.at[0, 0], lsem)

                @pl.when(fin_self)
                def _():
                    own.start()
                    own.wait()

                @pl.when(jnp.logical_not(fin_self))
                def _():
                    c = pltpu.make_async_remote_copy(
                        src_ref=wsend.at[0, 0], dst_ref=win.at[0, 0],
                        send_sem=ssem.at[number], recv_sem=rsem.at[number],
                        device_id=target, device_id_type=MESH,
                    )
                    c.start()
                    c.wait()

    for c in copies:
        c.wait_recv()
    blocks = []
    for j in range(2):
        w = (win[0, j] + win[1, j]) * (1.0 / 64.0)
        blocks.append(jnp.concatenate([w[:, 0:64], w[:, 64:128]], axis=0))
    first = jnp.where(y // 2 == k, y % 2, 1 - y % 2)
    o_ref[...] = jnp.where(
        first == 0,
        jnp.concatenate(blocks, axis=1),
        jnp.concatenate(blocks[::-1], axis=1),
    )
    for c in sends:
        c.wait_send()


def local(fields, factor):
    f32 = jnp.float32
    vmem = pl.BlockSpec(memory_space=pltpu.VMEM)
    return pl.pallas_call(
        kernel,
        out_shape=jax.ShapeDtypeStruct((64, 128), f32),
        in_specs=[vmem, pl.BlockSpec(memory_space=pl.ANY)],
        out_specs=vmem,
        scratch_shapes=[
            pltpu.VMEM((272, 128), f32),
            pltpu.VMEM((256, 128), f32),
            pltpu.VMEM((4, 2, 2, 64, 128), f32),
            pltpu.VMEM((3, 2, 2, 64, 128), f32),
            pltpu.VMEM((2, 2, 64, 128), f32),
            pltpu.VMEM((2, 64, 128), f32),
            pltpu.VMEM((2, 2, 2, 8, 128), f32),
            pltpu.VMEM((2, 4, 64, 256), f32),
            pltpu.VMEM((2, 2, 64, 256), f32),
            pltpu.VMEM((7, 128, 128), f32),
            pltpu.VMEM((7, 128, 128), f32),
            pltpu.VMEM((2, 2, 32, 128), f32),
            pltpu.VMEM((2, 2, 32, 128), f32),
            pltpu.SemaphoreType.DMA((3,)),
            pltpu.SemaphoreType.DMA((COPIES,)),
            pltpu.SemaphoreType.DMA((COPIES,)),
            pltpu.SemaphoreType.DMA,
        ],
        compiler_params=pltpu.CompilerParams(
            collective_id=0, has_side_effects=True, vmem_limit_bytes=32 << 20
        ),
        cost_estimate=pl.CostEstimate(flops=135_000_000, bytes_accessed=1_300_000, transcendentals=0),
    )(fields, factor)


def solution(mesh):
    in_specs = (P(None, "gz", "gy", "gx"), P())
    out_specs = P("gy", ("gx", "gz"))
    return jax.shard_map(local, mesh=mesh, in_specs=in_specs, out_specs=out_specs, check_vma=False)
```

```python
import jax
import jax.numpy as jnp
from jax import lax
from jax.experimental import pallas as pl
from jax.experimental.pallas import tpu as pltpu
from jax.sharding import PartitionSpec as P

MESH = pl.DeviceIdType.MESH
HIGHEST = lax.Precision.HIGHEST
NT = (((1,), (1,)), ((), ()))

XRS, ZHI, HALO, RZ, CA, RY, CY, PER = 0, 3, 4, 8, 11, 12, 16, 18
GRS, FIN, COPIES = 2 * PER, 2 * PER + 14, 2 * PER + 18


def smooth(p, length):
    return (
        p[0:length] + 4.0 * p[1 : length + 1] + 6.0 * p[2 : length + 2]
        + 4.0 * p[3 : length + 3] + p[4 : length + 4]
    ) * 0.0625


def beside(u):
    half = u.shape[0] // 2
    return jnp.concatenate([u[0:half], u[half:]], axis=1)


def kernel(
    f_ref, fac_ref, o_ref,
    fbuf, fac, sf, part, xin, tsum, zin, hin, rbuf, cbuf, gacc, gsend, gin, wsend, win,
    fsem, ssem, rsem, lsem,
):
    gx, gy, k = lax.axis_index("gx"), lax.axis_index("gy"), lax.axis_index("gz")
    h, x = gx // 4, gx % 4
    zlo, y = gy // 4, gy % 4
    a, m = zlo // 4, zlo % 4
    ye, yd = y + 1 - 2 * (y % 2), 3 - y

    def dev(h=h, x=x, a=a, m=m, y=y, k=k):
        return (h * 4 + x, (a * 4 + m) * 4 + y, k)

    x_peers = [(x + d) % 4 for d in range(1, 4)]
    m_peers = [(m + d) % 4 for d in range(1, 4)]
    g_peers = [((x + dx) % 4, (k + dk) % 2) for dx in range(4) for dk in range(2) if dx + dk]
    up, down = (gy + 1) % 32, (gy + 31) % 32
    fin_self = x == m

    lo = pl.multiple_of(jnp.maximum(gx * 256 - 8, 0), 8)
    mid = pl.multiple_of(gx * 256, 8)
    hi = pl.multiple_of(jnp.minimum(gx * 256 + 256, 2040), 8)
    loads = [
        pltpu.make_async_copy(fac_ref.at[pl.ds(lo, 8)], fac.at[pl.ds(0, 8)], fsem.at[0]),
        pltpu.make_async_copy(fac_ref.at[pl.ds(mid, 256)], fac.at[pl.ds(8, 256)], fsem.at[1]),
        pltpu.make_async_copy(fac_ref.at[pl.ds(hi, 8)], fac.at[pl.ds(264, 8)], fsem.at[2]),
    ]
    order = (2, 1, 3, 0)
    fields = {}
    for v in range(2):
        for i in range(4):
            xp = (x + order[i]) % 4
            fields[v, i] = pltpu.make_async_copy(
                f_ref.at[v, pl.ds(2 * xp, 2)], fbuf.at[v, i], fsem.at[3 + 4 * v + i]
            )
    for c in loads + list(fields.values()):
        c.start()

    barrier = pltpu.get_barrier_semaphore()

    def greet(d):
        pl.semaphore_signal(barrier, inc=1, device_id=d, device_id_type=MESH)

    for rel in (1, 0):
        hq = (h + rel) % 2
        greet((hq * 4 + x, up, k))
        greet((hq * 4 + x, down, k))
        greet(dev(h=hq, x=m, m=x, y=ye))
    greet(dev(h=1 - h, x=m, m=x))
    greet(dev(h=1 - h))
    greet(dev(a=1 - a))
    for mp in m_peers:
        greet(dev(m=mp))
    for xp, kp in g_peers:
        greet(dev(x=xp, k=kp))
    greet(dev(y=ye))
    greet(dev(y=yd))

    @pl.when(jnp.logical_not(fin_self))
    def _():
        greet(dev(x=m, m=x))

    for c in loads:
        c.wait()
    before = jnp.where(gx > 0, fac[6:8, :], 0.0)
    after = jnp.where(gx < 7, fac[264:266, :], 0.0)
    sf[...] = smooth(jnp.concatenate([before, fac[8:264, :], after], axis=0), 256)

    sends = []

    def send(src, dst, number, device):
        c = pltpu.make_async_remote_copy(
            src_ref=src, dst_ref=dst, send_sem=ssem.at[number], recv_sem=rsem.at[number],
            device_id=device, device_id_type=MESH,
        )
        c.start()
        sends.append(c)
        return c

    def project(v, i):
        fields[v, i].wait()
        part[v, i] = jnp.dot(
            fbuf[v, i].reshape(128, 256), sf[...],
            precision=HIGHEST, preferred_element_type=jnp.float32,
        ).reshape(2, 64, 128)

    xrs = [[], []]
    for v in range(2):
        for i in range(3):
            d = order[i]
            project(v, i)
            if v == 0 and i == 0:
                pl.semaphore_wait(barrier, jnp.where(fin_self, 21, 22))
            xrs[v].append(send(part.at[v, i], xin.at[v, i], PER * v + XRS + i, dev(x=x_peers[d - 1])))
        project(v, 3)

    zhi = [[], []]
    for v in range(2):
        for c in xrs[v]:
            c.wait_recv()
        tsum[v] = part[v, 3] + xin[v, 0] + xin[v, 1] + xin[v, 2]
        zhi[v].append(send(tsum.at[v, 1 - h], zin.at[v], PER * v + ZHI, dev(h=1 - h)))
        for rel in (1, 0):
            hq = (h + rel) % 2
            number = PER * v + HALO + rel
            zhi[v].append(
                send(tsum.at[v, hq, pl.ds(0, 8)], hin.at[v, 1, rel], number + 2, (hq * 4 + x, down, k))
            )
            zhi[v].append(
                send(tsum.at[v, hq, pl.ds(56, 8)], hin.at[v, 0, rel], number, (hq * 4 + x, up, k))
            )

    zs, far, ys = [[], []], [], [[], []]
    for v in range(2):
        base = PER * v
        for c in zhi[v]:
            c.wait_recv()
        before = jnp.where(gy > 0, hin[v, 0, 0, 6:8] + hin[v, 0, 1, 6:8], 0.0)
        after = jnp.where(gy < 31, hin[v, 1, 0, 0:2] + hin[v, 1, 1, 0:2], 0.0)
        own = tsum[v, h] + zin[v]
        block = smooth(jnp.concatenate([before, own, after], axis=0), 64)
        rbuf[v, 0, m] = block
        cbuf[v, a, 0] = block
        mine = rbuf.at[v, 0, m]
        far.append(send(mine, cbuf.at[v, a, 0], base + CA, dev(a=1 - a)))
        for d in range(3):
            zs[v].append(send(mine, rbuf.at[v, 0, m], base + RZ + d, dev(m=m_peers[d])))
        ys[v].append(send(mine, rbuf.at[v, 1, m], base + RY, dev(y=ye)))
        ys[v].append(send(mine, cbuf.at[v, a, 1], base + CY, dev(y=yd)))
    for v in range(2):
        base = PER * v
        for d in (0, 2, 1):
            zs[v][d].wait_recv()
            src = (m + 3 - d) % 4
            ys[v].append(send(rbuf.at[v, 0, src], rbuf.at[v, 1, src], base + RY + 1 + d, dev(y=ye)))
        far[v].wait_recv()
        ys[v].append(send(cbuf.at[v, 1 - a, 0], cbuf.at[v, 1 - a, 1], base + CY + 1, dev(y=yd)))

    def tile(v, mp, kp):
        jd = jnp.where(y // 2 == kp, 0, 1)
        rows = jnp.concatenate([rbuf[v, 0, mp], rbuf[v, 1, mp]], axis=0)
        cols = jnp.concatenate([cbuf[v, h, jd], cbuf[v, 1 - h, jd]], axis=0)
        return lax.dot_general(
            rows, cols, NT, precision=HIGHEST, preferred_element_type=jnp.float32
        )

    turn = (3, 4, 1, 2, 5, 6, 0)
    for c in ys[0]:
        c.wait_recv()
    for i in turn:
        gacc[i] = tile(0, *g_peers[i])
    gacc[7] = tile(0, x, k)
    for c in ys[1]:
        c.wait_recv()

    grs = [[], []]
    for i in turn:
        xp, kp = g_peers[i]
        t = gacc[i] + tile(1, xp, kp)
        gsend[1, i] = beside(t[:, 64:128])
        grs[1].append(send(gsend.at[1, i], gin.at[1, i], GRS + 7 + i, dev(x=xp, k=kp)))
        gsend[0, i] = beside(t[:, 0:64])
    for i in turn:
        xp, kp = g_peers[i]
        grs[0].append(send(gsend.at[0, i], gin.at[0, i], GRS + i, dev(x=xp, k=kp)))
    t = gacc[7] + tile(1, x, k)

    fin = []
    for rel in (1, 0):
        for c in grs[rel]:
            c.wait_recv()
        total = beside(t[:, 64 * rel : 64 * rel + 64])
        for i in range(7):
            total = total + gin[rel, i]
        aq = (h + rel) % 2
        for j in (1, 0):
            wsend[rel, j] = beside(total[:, j * 64 : (j + 1) * 64])
            target = dev(h=aq, x=m, m=x, y=ye if j else y)
            number = FIN + 2 * rel + j
            if rel or j:
                fin.append(send(wsend.at[rel, j], win.at[rel, j], number, target))
            else:
                own = pltpu.make_async_copy(wsend.at[0, 0], win.at[0, 0], lsem)

                @pl.when(fin_self)
                def _():
                    own.start()
                    own.wait()

                @pl.when(jnp.logical_not(fin_self))
                def _():
                    c = pltpu.make_async_remote_copy(
                        src_ref=wsend.at[0, 0], dst_ref=win.at[0, 0],
                        send_sem=ssem.at[number], recv_sem=rsem.at[number],
                        device_id=target, device_id_type=MESH,
                    )
                    c.start()
                    c.wait()

    for c in fin:
        c.wait_recv()
    blocks = []
    for j in range(2):
        w = (win[0, j] + win[1, j]) * (1.0 / 64.0)
        blocks.append(jnp.concatenate([w[:, 0:64], w[:, 64:128]], axis=0))
    first = jnp.where(y // 2 == k, y % 2, 1 - y % 2)
    o_ref[...] = jnp.where(
        first == 0,
        jnp.concatenate(blocks, axis=1),
        jnp.concatenate(blocks[::-1], axis=1),
    )
    for c in sends:
        c.wait_send()


def local(fields, factor):
    f32 = jnp.float32
    hbm = pl.BlockSpec(memory_space=pltpu.HBM)
    return pl.pallas_call(
        kernel,
        out_shape=jax.ShapeDtypeStruct((64, 128), f32),
        in_specs=[hbm, hbm],
        out_specs=pl.BlockSpec(memory_space=pltpu.VMEM),
        scratch_shapes=[
            pltpu.VMEM((2, 4, 2, 64, 256), f32),
            pltpu.VMEM((272, 128), f32),
            pltpu.VMEM((256, 128), f32),
            pltpu.VMEM((2, 4, 2, 64, 128), f32),
            pltpu.VMEM((2, 3, 2, 64, 128), f32),
            pltpu.VMEM((2, 2, 64, 128), f32),
            pltpu.VMEM((2, 64, 128), f32),
            pltpu.VMEM((2, 2, 2, 8, 128), f32),
            pltpu.VMEM((2, 2, 4, 64, 128), f32),
            pltpu.VMEM((2, 2, 2, 64, 128), f32),
            pltpu.VMEM((8, 128, 128), f32),
            pltpu.VMEM((2, 7, 64, 128), f32),
            pltpu.VMEM((2, 7, 64, 128), f32),
            pltpu.VMEM((2, 2, 32, 128), f32),
            pltpu.VMEM((2, 2, 32, 128), f32),
            pltpu.SemaphoreType.DMA((11,)),
            pltpu.SemaphoreType.DMA((COPIES,)),
            pltpu.SemaphoreType.DMA((COPIES,)),
            pltpu.SemaphoreType.DMA,
        ],
        compiler_params=pltpu.CompilerParams(
            collective_id=0, has_side_effects=True, vmem_limit_bytes=48 << 20
        ),
        cost_estimate=pl.CostEstimate(flops=135_000_000, bytes_accessed=1_300_000, transcendentals=0),
    )(fields, factor)


def solution(mesh):
    in_specs = (P(None, "gz", "gy", "gx"), P())
    out_specs = P("gy", ("gx", "gz"))
    return jax.shard_map(local, mesh=mesh, in_specs=in_specs, out_specs=out_specs, check_vma=False)
```

```python
import jax
import jax.numpy as jnp
from jax import lax
from jax.experimental import pallas as pl
from jax.experimental.pallas import tpu as pltpu
from jax.sharding import PartitionSpec as P

MESH = pl.DeviceIdType.MESH
HIGHEST = lax.Precision.HIGHEST
NT = (((1,), (1,)), ((), ()))

XRS, ZHI, HALO, RZ, CA, RY, CY, PER = 0, 3, 4, 8, 11, 12, 16, 18
GRS, FIN, COPIES = 2 * PER, 2 * PER + 14, 2 * PER + 18


def smooth(p, length):
    return (
        p[0:length] + 4.0 * p[1 : length + 1] + 6.0 * p[2 : length + 2]
        + 4.0 * p[3 : length + 3] + p[4 : length + 4]
    ) * 0.0625


def beside(u):
    half = u.shape[0] // 2
    return jnp.concatenate([u[0:half], u[half:]], axis=1)


def kernel(
    f_ref, fac_ref, o_ref,
    fbuf, fac, sf, part, xin, tsum, zin, hin, rbuf, cbuf, gacc, gsend, gin, wsend, win,
    fsem, ssem, rsem, reply,
):
    gx, gy, k = lax.axis_index("gx"), lax.axis_index("gy"), lax.axis_index("gz")
    h, x = gx // 4, gx % 4
    zlo, y = gy // 4, gy % 4
    a, m = zlo // 4, zlo % 4
    ye, yd = y + 1 - 2 * (y % 2), 3 - y

    def dev(h=h, x=x, a=a, m=m, y=y, k=k):
        return (h * 4 + x, (a * 4 + m) * 4 + y, k)

    x_peers = [(x + d) % 4 for d in range(1, 4)]
    m_peers = [(m + d) % 4 for d in range(1, 4)]
    g_peers = [((x + dx) % 4, (k + dk) % 2) for dx in range(4) for dk in range(2) if dx + dk]
    up, down = (gy + 1) % 32, (gy + 31) % 32
    has_up, has_down = gy < 31, gy > 0
    sides = jnp.where(has_up, 1, 0) + jnp.where(has_down, 1, 0)

    lo = pl.multiple_of(jnp.maximum(gx * 256 - 8, 0), 8)
    mid = pl.multiple_of(gx * 256, 8)
    hi = pl.multiple_of(jnp.minimum(gx * 256 + 256, 2040), 8)
    loads = [
        pltpu.make_async_copy(fac_ref.at[pl.ds(lo, 8)], fac.at[pl.ds(0, 8)], fsem.at[0]),
        pltpu.make_async_copy(fac_ref.at[pl.ds(mid, 256)], fac.at[pl.ds(8, 256)], fsem.at[1]),
        pltpu.make_async_copy(fac_ref.at[pl.ds(hi, 8)], fac.at[pl.ds(264, 8)], fsem.at[2]),
    ]
    order = (2, 1, 3, 0)
    fields = {}
    for v in range(2):
        for i in range(4):
            xp = (x + order[i]) % 4
            fields[v, i] = pltpu.make_async_copy(
                f_ref.at[v, pl.ds(2 * xp, 2)], fbuf.at[v, i], fsem.at[3 + 4 * v + i]
            )
    for c in loads + list(fields.values()):
        c.start()

    hin[...] = jnp.zeros_like(hin)
    barrier = pltpu.get_barrier_semaphore()

    def greet(d, semaphore=barrier, when=None):
        def tell():
            pl.semaphore_signal(semaphore, inc=1, device_id=d, device_id_type=MESH)

        if when is None:
            tell()
        else:
            pl.when(when)(tell)

    greet(dev(h=1), when=h == 0)
    greet((4 + x, up, k), when=(h == 0) & has_up)
    greet((4 + x, down, k), when=(h == 0) & has_down)
    greet(dev(a=1), when=a == 0)
    for mp in m_peers:
        greet(dev(m=mp), when=mp > m)
    for xp, kp in g_peers:
        greet(dev(x=xp, k=kp))
    greet(dev(y=ye))
    greet(dev(y=yd))
    greet((gx, up, k), when=has_up)
    greet((gx, down, k), when=has_down)

    for c in loads:
        c.wait()
    before = jnp.where(gx > 0, fac[6:8, :], 0.0)
    after = jnp.where(gx < 7, fac[264:266, :], 0.0)
    sf[...] = smooth(jnp.concatenate([before, fac[8:264, :], after], axis=0), 256)

    sends = []

    def send(src, dst, number, device, when=None):
        c = pltpu.make_async_remote_copy(
            src_ref=src, dst_ref=dst, send_sem=ssem.at[number], recv_sem=rsem.at[number],
            device_id=device, device_id_type=MESH,
        )
        if when is None:
            c.start()
        else:
            pl.when(when)(c.start)
        sends.append((c, when))
        return c

    def project(v, i):
        fields[v, i].wait()
        part[v, i] = jnp.dot(
            fbuf[v, i].reshape(128, 256), sf[...],
            precision=HIGHEST, preferred_element_type=jnp.float32,
        ).reshape(2, 64, 128)

    xrs = [[], []]
    for v in range(2):
        for i in range(3):
            d = order[i]
            project(v, i)
            if v == 0 and i == 0:
                pl.semaphore_wait(barrier, 9 + sides + m + a + h * (1 + sides))
            xrs[v].append(send(part.at[v, i], xin.at[v, i], PER * v + XRS + i, dev(x=x_peers[d - 1])))
        if v == 0:
            for mp in m_peers:
                greet(dev(m=mp), reply, mp < m)
            greet(dev(a=0), reply, a == 1)
            greet(dev(h=0), reply, h == 1)
            greet((x, up, k), reply, (h == 1) & has_up)
            greet((x, down, k), reply, (h == 1) & has_down)
        project(v, 3)

    zhi, halos = [], [[], []]
    replies = 3 - m + 1 - a + (1 - h) * (1 + sides)
    for v in range(2):
        for c in xrs[v]:
            c.wait_recv()
        tsum[v] = part[v, 3] + xin[v, 0] + xin[v, 1] + xin[v, 2]
        if v == 0:

            @pl.when(replies > 0)
            def _():
                pl.semaphore_wait(reply, replies)

        zhi.append(send(tsum.at[v, 1 - h], zin.at[v], PER * v + ZHI, dev(h=1 - h)))
        for rel in (1, 0):
            hq = (h + rel) % 2
            number = PER * v + HALO + rel
            low = tsum.at[v, hq, pl.ds(0, 8)]
            c = send(low, hin.at[v, 1, rel], number + 2, (hq * 4 + x, down, k), has_down)
            halos[v].append((c, has_up))
            high = tsum.at[v, hq, pl.ds(56, 8)]
            c = send(high, hin.at[v, 0, rel], number, (hq * 4 + x, up, k), has_up)
            halos[v].append((c, has_down))

    zs, far, ys = [[], []], [], [[], []]
    for v in range(2):
        base = PER * v
        zhi[v].wait_recv()
        for c, when in halos[v]:
            pl.when(when)(c.wait_recv)
        before = hin[v, 0, 0, 6:8] + hin[v, 0, 1, 6:8]
        after = hin[v, 1, 0, 0:2] + hin[v, 1, 1, 0:2]
        own = tsum[v, h] + zin[v]
        block = smooth(jnp.concatenate([before, own, after], axis=0), 64)
        rbuf[v, 0, m] = block
        cbuf[v, a, 0] = block
        mine = rbuf.at[v, 0, m]
        for d in range(3):
            zs[v].append(send(mine, rbuf.at[v, 0, m], base + RZ + d, dev(m=m_peers[d])))
        ys[v].append(send(mine, rbuf.at[v, 1, m], base + RY, dev(y=ye)))
        ys[v].append(send(mine, cbuf.at[v, a, 1], base + CY, dev(y=yd)))
        far.append(send(mine, cbuf.at[v, a, 0], base + CA, dev(a=1 - a)))
    turned = []

    def turn_far(v):
        far[v].wait_recv()
        there = cbuf.at[v, 1 - a]
        turned.append(send(there.at[0], there.at[1], PER * v + CY + 1, dev(y=yd)))

    for v in range(2):
        base = PER * v
        for d in (0, 2, 1):
            zs[v][d].wait_recv()
            src = (m + 3 - d) % 4
            ys[v].append(send(rbuf.at[v, 0, src], rbuf.at[v, 1, src], base + RY + 1 + d, dev(y=ye)))
        if v == 0:
            turn_far(0)

    jd = jnp.where(y // 2 == k, 0, 1)

    def tile(v, mp, half):
        aq = 1 - a if half else a
        rows = jnp.concatenate([rbuf[v, 0, mp], rbuf[v, 1, mp]], axis=0)
        cols = jnp.concatenate([cbuf[v, aq, jd], cbuf[v, aq, 1 - jd]], axis=0)
        return lax.dot_general(
            rows, cols, NT, precision=HIGHEST, preferred_element_type=jnp.float32
        )

    def scatter(half):
        copies = []
        for dx in (2, 1, 3, 0):
            t = gacc[half, dx] + tile(1, (x + dx) % 4, half)
            for dk in (0, 1):
                i = 2 * dx - 1 + dk
                piece = beside(t[:, 64 * dk : 64 * dk + 64])
                if i < 0:
                    own = piece
                else:
                    xp, kp = g_peers[i]
                    gsend[half, i] = piece
                    number = GRS + 7 * half + i
                    copies.append(send(gsend.at[half, i], gin.at[half, i], number, dev(x=xp, k=kp)))
        return own, copies

    def deliver(half, own, copies):
        for c in copies:
            c.wait_recv()
        total = own
        for i in range(7):
            total = total + gin[half, i]
        aq = 1 - a if half else a
        rel = (h + aq) % 2
        for j in (1, 0):
            packed = beside(total[:, j * 64 : (j + 1) * 64])
            wsend[half, j] = packed
            target = dev(h=aq, x=m, m=x, y=ye if j else y)
            away = None if j else (x != m) | (rel != 0)
            send(wsend.at[half, j], win.at[rel, j], FIN + 2 * rel + j, target, away)
            if j == 0:

                @pl.when(jnp.logical_not(away))
                def _():
                    win[0, 0] = packed

    for c in ys[0]:
        c.wait_recv()
    for dx in range(4):
        gacc[0, dx] = tile(0, (x + dx) % 4, 0)
    for c in ys[1]:
        c.wait_recv()
    first_half = scatter(0)
    turn_far(1)
    turned[0].wait_recv()
    for dx in range(4):
        gacc[1, dx] = tile(0, (x + dx) % 4, 1)
    turned[1].wait_recv()
    second_half = scatter(1)
    deliver(0, *first_half)
    deliver(1, *second_half)

    for rel in range(2):
        for j in range(2):
            number = FIN + 2 * rel + j
            c = pltpu.make_async_remote_copy(
                src_ref=wsend.at[rel, j], dst_ref=win.at[rel, j],
                send_sem=ssem.at[number], recv_sem=rsem.at[number],
                device_id=dev(x=m, m=x, h=(h + rel) % 2, y=ye if j else y), device_id_type=MESH,
            )
            if rel or j:
                c.wait_recv()
            else:
                pl.when(x != m)(c.wait_recv)
    blocks = []
    for j in range(2):
        w = (win[0, j] + win[1, j]) * (1.0 / 64.0)
        blocks.append(jnp.concatenate([w[:, 0:64], w[:, 64:128]], axis=0))
    first = jnp.where(y // 2 == k, y % 2, 1 - y % 2)
    o_ref[...] = jnp.where(
        first == 0,
        jnp.concatenate(blocks, axis=1),
        jnp.concatenate(blocks[::-1], axis=1),
    )
    for c, when in sends:
        if when is None:
            c.wait_send()
        else:
            pl.when(when)(c.wait_send)


def local(fields, factor):
    f32 = jnp.float32
    hbm = pl.BlockSpec(memory_space=pltpu.HBM)
    return pl.pallas_call(
        kernel,
        out_shape=jax.ShapeDtypeStruct((64, 128), f32),
        in_specs=[hbm, hbm],
        out_specs=pl.BlockSpec(memory_space=pltpu.VMEM),
        scratch_shapes=[
            pltpu.VMEM((2, 4, 2, 64, 256), f32),
            pltpu.VMEM((272, 128), f32),
            pltpu.VMEM((256, 128), f32),
            pltpu.VMEM((2, 4, 2, 64, 128), f32),
            pltpu.VMEM((2, 3, 2, 64, 128), f32),
            pltpu.VMEM((2, 2, 64, 128), f32),
            pltpu.VMEM((2, 64, 128), f32),
            pltpu.VMEM((2, 2, 2, 8, 128), f32),
            pltpu.VMEM((2, 2, 4, 64, 128), f32),
            pltpu.VMEM((2, 2, 2, 64, 128), f32),
            pltpu.VMEM((2, 4, 128, 128), f32),
            pltpu.VMEM((2, 7, 64, 128), f32),
            pltpu.VMEM((2, 7, 64, 128), f32),
            pltpu.VMEM((2, 2, 32, 128), f32),
            pltpu.VMEM((2, 2, 32, 128), f32),
            pltpu.SemaphoreType.DMA((11,)),
            pltpu.SemaphoreType.DMA((COPIES,)),
            pltpu.SemaphoreType.DMA((COPIES,)),
            pltpu.SemaphoreType.REGULAR,
        ],
        compiler_params=pltpu.CompilerParams(
            collective_id=0, has_side_effects=True, vmem_limit_bytes=60 << 20
        ),
        cost_estimate=pl.CostEstimate(flops=135_000_000, bytes_accessed=1_300_000, transcendentals=0),
    )(fields, factor)


def solution(mesh):
    in_specs = (P(None, "gz", "gy", "gx"), P())
    out_specs = P("gy", ("gx", "gz"))
    return jax.shard_map(local, mesh=mesh, in_specs=in_specs, out_specs=out_specs, check_vma=False)
```

```python
import jax
import jax.numpy as jnp
from jax import lax
from jax.experimental import pallas as pl
from jax.experimental.pallas import tpu as pltpu
from jax.sharding import PartitionSpec as P

MESH = pl.DeviceIdType.MESH
HIGHEST = lax.Precision.HIGHEST
NT = (((1,), (1,)), ((), ()))

XRS, ZHI, HALO, RZ, CA, RY, CY, PER = 0, 3, 4, 8, 11, 12, 16, 18
GRS, FIN, COPIES = 2 * PER, 2 * PER + 14, 2 * PER + 18


def smooth(p, length):
    return (
        p[0:length] + 4.0 * p[1 : length + 1] + 6.0 * p[2 : length + 2]
        + 4.0 * p[3 : length + 3] + p[4 : length + 4]
    ) * 0.0625


def beside(u):
    half = u.shape[0] // 2
    return jnp.concatenate([u[0:half], u[half:]], axis=1)


def kernel(
    f_ref, fac_ref, o_ref,
    fbuf, fac, sf, part, xin, tsum, zin, hin, rbuf, cbuf, gacc, gsend, gin, wsend, win,
    fsem, ssem, rsem, reply,
):
    gx, gy, k = lax.axis_index("gx"), lax.axis_index("gy"), lax.axis_index("gz")
    h, x = gx // 4, gx % 4
    zlo, y = gy // 4, gy % 4
    a, m = zlo // 4, zlo % 4
    ye, yd = y + 1 - 2 * (y % 2), 3 - y

    def dev(h=h, x=x, a=a, m=m, y=y, k=k):
        return (h * 4 + x, (a * 4 + m) * 4 + y, k)

    x_peers = [(x + d) % 4 for d in range(1, 4)]
    m_peers = [(m + d) % 4 for d in range(1, 4)]
    g_peers = [((x + dx) % 4, (k + dk) % 2) for dx in range(4) for dk in range(2) if dx + dk]
    up, down = (gy + 1) % 32, (gy + 31) % 32
    has_up, has_down = gy < 31, gy > 0
    sides = jnp.where(has_up, 1, 0) + jnp.where(has_down, 1, 0)

    lo = pl.multiple_of(jnp.maximum(gx * 256 - 8, 0), 8)
    mid = pl.multiple_of(gx * 256, 8)
    hi = pl.multiple_of(jnp.minimum(gx * 256 + 256, 2040), 8)
    loads = [
        pltpu.make_async_copy(fac_ref.at[pl.ds(lo, 8)], fac.at[pl.ds(0, 8)], fsem.at[0]),
        pltpu.make_async_copy(fac_ref.at[pl.ds(mid, 256)], fac.at[pl.ds(8, 256)], fsem.at[1]),
        pltpu.make_async_copy(fac_ref.at[pl.ds(hi, 8)], fac.at[pl.ds(264, 8)], fsem.at[2]),
    ]
    order = (2, 1, 3, 0)
    fields = {}
    for v in range(2):
        for i in range(4):
            xp = (x + order[i]) % 4
            fields[v, i] = pltpu.make_async_copy(
                f_ref.at[v, pl.ds(2 * xp, 2)], fbuf.at[v, i], fsem.at[3 + 4 * v + i]
            )
    for c in loads + list(fields.values()):
        c.start()

    hin[...] = jnp.zeros_like(hin)
    barrier = pltpu.get_barrier_semaphore()

    def greet(d, semaphore=barrier, when=None):
        def tell():
            pl.semaphore_signal(semaphore, inc=1, device_id=d, device_id_type=MESH)

        if when is None:
            tell()
        else:
            pl.when(when)(tell)

    greet(dev(h=1), when=h == 0)
    greet((4 + x, up, k), when=(h == 0) & has_up)
    greet((4 + x, down, k), when=(h == 0) & has_down)
    greet(dev(a=1), when=a == 0)
    for mp in m_peers:
        greet(dev(m=mp), when=mp > m)
    for xp, kp in g_peers:
        greet(dev(x=xp, k=kp))
    greet(dev(y=ye))
    greet(dev(y=yd))
    greet((gx, up, k), when=has_up)
    greet((gx, down, k), when=has_down)

    for c in loads:
        c.wait()
    before = jnp.where(gx > 0, fac[6:8, :], 0.0)
    after = jnp.where(gx < 7, fac[264:266, :], 0.0)
    sf[...] = smooth(jnp.concatenate([before, fac[8:264, :], after], axis=0), 256)

    sends = []

    def send(src, dst, number, device, when=None):
        c = pltpu.make_async_remote_copy(
            src_ref=src, dst_ref=dst, send_sem=ssem.at[number], recv_sem=rsem.at[number],
            device_id=device, device_id_type=MESH,
        )
        if when is None:
            c.start()
        else:
            pl.when(when)(c.start)
        sends.append((c, when))
        return c

    def project(v, i):
        fields[v, i].wait()
        part[v, i] = jnp.dot(
            fbuf[v, i].reshape(128, 256), sf[...],
            precision=HIGHEST, preferred_element_type=jnp.float32,
        ).reshape(2, 64, 128)

    xrs = [[], []]
    for v in range(2):
        for i in range(3):
            d = order[i]
            project(v, i)
            if v == 0 and i == 0:
                pl.semaphore_wait(barrier, 9 + sides + m + a + h * (1 + sides))
            xrs[v].append(send(part.at[v, i], xin.at[v, i], PER * v + XRS + i, dev(x=x_peers[d - 1])))
        if v == 0:
            for mp in m_peers:
                greet(dev(m=mp), reply, mp < m)
            greet(dev(a=0), reply, a == 1)
            greet(dev(h=0), reply, h == 1)
            greet((x, up, k), reply, (h == 1) & has_up)
            greet((x, down, k), reply, (h == 1) & has_down)
        project(v, 3)

    zhi, halos = [], [[], []]
    replies = 3 - m + 1 - a + (1 - h) * (1 + sides)
    for v in range(2):
        for c in xrs[v]:
            c.wait_recv()
        tsum[v] = part[v, 3] + xin[v, 0] + xin[v, 1] + xin[v, 2]
        if v == 0:

            @pl.when(replies > 0)
            def _():
                pl.semaphore_wait(reply, replies)

        for rel in (1, 0):
            hq = (h + rel) % 2
            number = PER * v + HALO + rel
            low = tsum.at[v, hq, pl.ds(0, 8)]
            c = send(low, hin.at[v, 1, rel], number + 2, (hq * 4 + x, down, k), has_down)
            halos[v].append((c, has_up))
            high = tsum.at[v, hq, pl.ds(56, 8)]
            c = send(high, hin.at[v, 0, rel], number, (hq * 4 + x, up, k), has_up)
            halos[v].append((c, has_down))
        zhi.append(send(tsum.at[v, 1 - h], zin.at[v], PER * v + ZHI, dev(h=1 - h)))

    zs, far, ys = [[], []], [], [[], []]
    for v in range(2):
        base = PER * v
        zhi[v].wait_recv()
        for c, when in halos[v]:
            pl.when(when)(c.wait_recv)
        before = hin[v, 0, 0, 6:8] + hin[v, 0, 1, 6:8]
        after = hin[v, 1, 0, 0:2] + hin[v, 1, 1, 0:2]
        own = tsum[v, h] + zin[v]
        block = smooth(jnp.concatenate([before, own, after], axis=0), 64)
        rbuf[v, 0, m] = block
        cbuf[v, a, 0] = block
        mine = rbuf.at[v, 0, m]
        for d in range(3):
            zs[v].append(send(mine, rbuf.at[v, 0, m], base + RZ + d, dev(m=m_peers[d])))
        ys[v].append(send(mine, rbuf.at[v, 1, m], base + RY, dev(y=ye)))
        ys[v].append(send(mine, cbuf.at[v, a, 1], base + CY, dev(y=yd)))
        far.append(send(mine, cbuf.at[v, a, 0], base + CA, dev(a=1 - a)))
    turned = []

    def turn_far(v):
        far[v].wait_recv()
        there = cbuf.at[v, 1 - a]
        turned.append(send(there.at[0], there.at[1], PER * v + CY + 1, dev(y=yd)))

    for v in range(2):
        base = PER * v
        for d in (0, 2, 1):
            zs[v][d].wait_recv()
            src = (m + 3 - d) % 4
            ys[v].append(send(rbuf.at[v, 0, src], rbuf.at[v, 1, src], base + RY + 1 + d, dev(y=ye)))
        if v == 0:
            turn_far(0)

    jd = jnp.where(y // 2 == k, 0, 1)

    def tile(v, mp, half):
        aq = 1 - a if half else a
        rows = jnp.concatenate([rbuf[v, 0, mp], rbuf[v, 1, mp]], axis=0)
        cols = jnp.concatenate([cbuf[v, aq, jd], cbuf[v, aq, 1 - jd]], axis=0)
        return lax.dot_general(
            rows, cols, NT, precision=HIGHEST, preferred_element_type=jnp.float32
        )

    def scatter(half):
        copies = []
        for dx in (2, 1, 3, 0):
            t = gacc[half, dx] + tile(1, (x + dx) % 4, half)
            for dk in (0, 1):
                i = 2 * dx - 1 + dk
                piece = beside(t[:, 64 * dk : 64 * dk + 64])
                if i < 0:
                    own = piece
                else:
                    xp, kp = g_peers[i]
                    gsend[half, i] = piece
                    number = GRS + 7 * half + i
                    copies.append(send(gsend.at[half, i], gin.at[half, i], number, dev(x=xp, k=kp)))
        return own, copies

    def deliver(half, own, copies):
        for c in copies:
            c.wait_recv()
        total = own
        for i in range(7):
            total = total + gin[half, i]
        aq = 1 - a if half else a
        rel = (h + aq) % 2
        for j in (1, 0):
            packed = beside(total[:, j * 64 : (j + 1) * 64])
            wsend[half, j] = packed
            target = dev(h=aq, x=m, m=x, y=ye if j else y)
            away = None if j else (x != m) | (rel != 0)
            send(wsend.at[half, j], win.at[rel, j], FIN + 2 * rel + j, target, away)
            if j == 0:

                @pl.when(jnp.logical_not(away))
                def _():
                    win[0, 0] = packed

    for c in ys[0]:
        c.wait_recv()
    for dx in range(4):
        gacc[0, dx] = tile(0, (x + dx) % 4, 0)
    for c in ys[1]:
        c.wait_recv()
    first_half = scatter(0)
    turn_far(1)
    turned[0].wait_recv()
    for dx in range(4):
        gacc[1, dx] = tile(0, (x + dx) % 4, 1)
    turned[1].wait_recv()
    second_half = scatter(1)
    deliver(0, *first_half)
    deliver(1, *second_half)

    for rel in range(2):
        for j in range(2):
            number = FIN + 2 * rel + j
            c = pltpu.make_async_remote_copy(
                src_ref=wsend.at[rel, j], dst_ref=win.at[rel, j],
                send_sem=ssem.at[number], recv_sem=rsem.at[number],
                device_id=dev(x=m, m=x, h=(h + rel) % 2, y=ye if j else y), device_id_type=MESH,
            )
            if rel or j:
                c.wait_recv()
            else:
                pl.when(x != m)(c.wait_recv)
    blocks = []
    for j in range(2):
        w = (win[0, j] + win[1, j]) * (1.0 / 64.0)
        blocks.append(jnp.concatenate([w[:, 0:64], w[:, 64:128]], axis=0))
    first = jnp.where(y // 2 == k, y % 2, 1 - y % 2)
    o_ref[...] = jnp.where(
        first == 0,
        jnp.concatenate(blocks, axis=1),
        jnp.concatenate(blocks[::-1], axis=1),
    )
    for c, when in sends:
        if when is None:
            c.wait_send()
        else:
            pl.when(when)(c.wait_send)


def local(fields, factor):
    f32 = jnp.float32
    hbm = pl.BlockSpec(memory_space=pltpu.HBM)
    return pl.pallas_call(
        kernel,
        out_shape=jax.ShapeDtypeStruct((64, 128), f32),
        in_specs=[hbm, hbm],
        out_specs=pl.BlockSpec(memory_space=pltpu.VMEM),
        scratch_shapes=[
            pltpu.VMEM((2, 4, 2, 64, 256), f32),
            pltpu.VMEM((272, 128), f32),
            pltpu.VMEM((256, 128), f32),
            pltpu.VMEM((2, 4, 2, 64, 128), f32),
            pltpu.VMEM((2, 3, 2, 64, 128), f32),
            pltpu.VMEM((2, 2, 64, 128), f32),
            pltpu.VMEM((2, 64, 128), f32),
            pltpu.VMEM((2, 2, 2, 8, 128), f32),
            pltpu.VMEM((2, 2, 4, 64, 128), f32),
            pltpu.VMEM((2, 2, 2, 64, 128), f32),
            pltpu.VMEM((2, 4, 128, 128), f32),
            pltpu.VMEM((2, 7, 64, 128), f32),
            pltpu.VMEM((2, 7, 64, 128), f32),
            pltpu.VMEM((2, 2, 32, 128), f32),
            pltpu.VMEM((2, 2, 32, 128), f32),
            pltpu.SemaphoreType.DMA((11,)),
            pltpu.SemaphoreType.DMA((COPIES,)),
            pltpu.SemaphoreType.DMA((COPIES,)),
            pltpu.SemaphoreType.REGULAR,
        ],
        compiler_params=pltpu.CompilerParams(
            collective_id=0, has_side_effects=True, vmem_limit_bytes=60 << 20
        ),
        cost_estimate=pl.CostEstimate(flops=135_000_000, bytes_accessed=1_300_000, transcendentals=0),
    )(fields, factor)


def solution(mesh):
    in_specs = (P(None, "gz", "gy", "gx"), P())
    out_specs = P("gy", ("gx", "gz"))
    return jax.shard_map(local, mesh=mesh, in_specs=in_specs, out_specs=out_specs, check_vma=False)
```

```python
import jax
import jax.numpy as jnp
from jax import lax
from jax.experimental import pallas as pl
from jax.experimental.pallas import tpu as pltpu
from jax.sharding import PartitionSpec as P

MESH = pl.DeviceIdType.MESH
HIGHEST = lax.Precision.HIGHEST
NT = (((1,), (1,)), ((), ()))

XRS, ZHI, HALO, RZ, CA, RY, CY, PER = 0, 3, 4, 8, 11, 12, 16, 18
GRS, FIN, COPIES = 2 * PER, 2 * PER + 14, 2 * PER + 18


def smooth(p, length):
    return (
        p[0:length] + 4.0 * p[1 : length + 1] + 6.0 * p[2 : length + 2]
        + 4.0 * p[3 : length + 3] + p[4 : length + 4]
    ) * 0.0625


def beside(u):
    half = u.shape[0] // 2
    return jnp.concatenate([u[0:half], u[half:]], axis=1)


def kernel(
    f_ref, fac_ref, o_ref,
    fbuf, fac, sf, part, xin, tsum, zin, hin, rbuf, cbuf, gacc, gsend, gin, wsend, win,
    fsem, ssem, rsem, reply,
):
    gx, gy, k = lax.axis_index("gx"), lax.axis_index("gy"), lax.axis_index("gz")
    h, x = gx // 4, gx % 4
    zlo, y = gy // 4, gy % 4
    a, m = zlo // 4, zlo % 4
    ye, yd = y + 1 - 2 * (y % 2), 3 - y

    def dev(h=h, x=x, a=a, m=m, y=y, k=k):
        return (h * 4 + x, (a * 4 + m) * 4 + y, k)

    x_peers = [(x + d) % 4 for d in range(1, 4)]
    m_peers = [(m + d) % 4 for d in range(1, 4)]
    g_peers = [((x + dx) % 4, (k + dk) % 2) for dx in range(4) for dk in range(2) if dx + dk]
    up, down = (gy + 1) % 32, (gy + 31) % 32
    has_up, has_down = gy < 31, gy > 0
    sides = jnp.where(has_up, 1, 0) + jnp.where(has_down, 1, 0)

    lo = pl.multiple_of(jnp.maximum(gx * 256 - 8, 0), 8)
    mid = pl.multiple_of(gx * 256, 8)
    hi = pl.multiple_of(jnp.minimum(gx * 256 + 256, 2040), 8)
    loads = [
        pltpu.make_async_copy(fac_ref.at[pl.ds(lo, 8)], fac.at[pl.ds(0, 8)], fsem.at[0]),
        pltpu.make_async_copy(fac_ref.at[pl.ds(mid, 256)], fac.at[pl.ds(8, 256)], fsem.at[1]),
        pltpu.make_async_copy(fac_ref.at[pl.ds(hi, 8)], fac.at[pl.ds(264, 8)], fsem.at[2]),
    ]
    order = (2, 1, 3, 0)
    fields = {}
    for v in range(2):
        for i in range(4):
            xp = (x + order[i]) % 4
            fields[v, i] = pltpu.make_async_copy(
                f_ref.at[v, pl.ds(2 * xp, 2)], fbuf.at[v, i], fsem.at[3 + 4 * v + i]
            )
    for c in loads + list(fields.values()):
        c.start()

    hin[...] = jnp.zeros_like(hin)
    barrier = pltpu.get_barrier_semaphore()

    def greet(d, semaphore=barrier, when=None):
        def tell():
            pl.semaphore_signal(semaphore, inc=1, device_id=d, device_id_type=MESH)

        if when is None:
            tell()
        else:
            pl.when(when)(tell)

    greet(dev(h=1), when=h == 0)
    greet((4 + x, up, k), when=(h == 0) & has_up)
    greet((4 + x, down, k), when=(h == 0) & has_down)
    greet(dev(a=1), when=a == 0)
    for mp in m_peers:
        greet(dev(m=mp), when=mp > m)
    for xp, kp in g_peers:
        greet(dev(x=xp, k=kp))
    greet(dev(y=ye))
    greet(dev(y=yd))
    greet((gx, up, k), when=has_up)
    greet((gx, down, k), when=has_down)

    for c in loads:
        c.wait()
    before = jnp.where(gx > 0, fac[6:8, :], 0.0)
    after = jnp.where(gx < 7, fac[264:266, :], 0.0)
    sf[...] = smooth(jnp.concatenate([before, fac[8:264, :], after], axis=0), 256)

    sends = []

    def send(src, dst, number, device, when=None):
        c = pltpu.make_async_remote_copy(
            src_ref=src, dst_ref=dst, send_sem=ssem.at[number], recv_sem=rsem.at[number],
            device_id=device, device_id_type=MESH,
        )
        if when is None:
            c.start()
        else:
            pl.when(when)(c.start)
        sends.append((c, when))
        return c

    def project(v, i):
        fields[v, i].wait()
        part[v, i] = jnp.dot(
            fbuf[v, i].reshape(128, 256), sf[...],
            precision=HIGHEST, preferred_element_type=jnp.float32,
        ).reshape(2, 64, 128)

    xrs = [[], []]
    for v in range(2):
        for i in range(3):
            d = order[i]
            project(v, i)
            if v == 0 and i == 0:
                pl.semaphore_wait(barrier, 9 + sides + m + a + h * (1 + sides))
            xrs[v].append(send(part.at[v, i], xin.at[v, i], PER * v + XRS + i, dev(x=x_peers[d - 1])))
        if v == 0:
            for mp in m_peers:
                greet(dev(m=mp), reply, mp < m)
            greet(dev(a=0), reply, a == 1)
            greet(dev(h=0), reply, h == 1)
            greet((x, up, k), reply, (h == 1) & has_up)
            greet((x, down, k), reply, (h == 1) & has_down)
        project(v, 3)

    zhi, halos = [], [[], []]
    replies = 3 - m + 1 - a + (1 - h) * (1 + sides)
    for v in range(2):
        for c in xrs[v]:
            c.wait_recv()
        tsum[v] = part[v, 3] + xin[v, 0] + xin[v, 1] + xin[v, 2]
        if v == 0:

            @pl.when(replies > 0)
            def _():
                pl.semaphore_wait(reply, replies)

        for rel in (1, 0):
            hq = (h + rel) % 2
            number = PER * v + HALO + rel
            low = tsum.at[v, hq, pl.ds(0, 8)]
            c = send(low, hin.at[v, 1, rel], number + 2, (hq * 4 + x, down, k), has_down)
            halos[v].append((c, has_up))
            high = tsum.at[v, hq, pl.ds(56, 8)]
            c = send(high, hin.at[v, 0, rel], number, (hq * 4 + x, up, k), has_up)
            halos[v].append((c, has_down))
        zhi.append(send(tsum.at[v, 1 - h], zin.at[v], PER * v + ZHI, dev(h=1 - h)))

    zs, far, ys = [[], []], [], [[], []]
    for v in range(2):
        base = PER * v
        zhi[v].wait_recv()
        for c, when in halos[v]:
            pl.when(when)(c.wait_recv)
        before = hin[v, 0, 0, 6:8] + hin[v, 0, 1, 6:8]
        after = hin[v, 1, 0, 0:2] + hin[v, 1, 1, 0:2]
        own = tsum[v, h] + zin[v]
        block = smooth(jnp.concatenate([before, own, after], axis=0), 64)
        rbuf[v, 0, m] = block
        cbuf[v, a, 0] = block
        mine = rbuf.at[v, 0, m]
        for d in range(3):
            zs[v].append(send(mine, rbuf.at[v, 0, m], base + RZ + d, dev(m=m_peers[d])))
        ys[v].append(send(mine, rbuf.at[v, 1, m], base + RY, dev(y=ye)))
        ys[v].append(send(mine, cbuf.at[v, a, 1], base + CY, dev(y=yd)))
        far.append(send(mine, cbuf.at[v, a, 0], base + CA, dev(a=1 - a)))
    turned = []

    def turn_far(v):
        far[v].wait_recv()
        there = cbuf.at[v, 1 - a]
        turned.append(send(there.at[0], there.at[1], PER * v + CY + 1, dev(y=yd)))

    for v in range(2):
        base = PER * v
        for d in (0, 2, 1):
            zs[v][d].wait_recv()
            src = (m + 3 - d) % 4
            ys[v].append(send(rbuf.at[v, 0, src], rbuf.at[v, 1, src], base + RY + 1 + d, dev(y=ye)))
        if v == 0:
            turn_far(0)

    jd = jnp.where(y // 2 == k, 0, 1)

    def tile(v, mp, half):
        aq = 1 - a if half else a
        rows = jnp.concatenate([rbuf[v, 0, mp], rbuf[v, 1, mp]], axis=0)
        cols = jnp.concatenate([cbuf[v, aq, jd], cbuf[v, aq, 1 - jd]], axis=0)
        return lax.dot_general(
            rows, cols, NT, precision=HIGHEST, preferred_element_type=jnp.float32
        )

    def scatter(half):
        copies = []
        for dx in (2, 1, 3, 0):
            t = gacc[half, dx] + tile(1, (x + dx) % 4, half)
            for dk in (0, 1):
                i = 2 * dx - 1 + dk
                piece = beside(t[:, 64 * dk : 64 * dk + 64])
                if i < 0:
                    own = piece
                else:
                    xp, kp = g_peers[i]
                    gsend[half, i] = piece
                    number = GRS + 7 * half + i
                    copies.append(send(gsend.at[half, i], gin.at[half, i], number, dev(x=xp, k=kp)))
        return own, copies

    def deliver(half, own, copies):
        for c in copies:
            c.wait_recv()
        total = own
        for i in range(7):
            total = total + gin[half, i]
        aq = 1 - a if half else a
        rel = (h + aq) % 2
        for j in (1, 0):
            packed = beside(total[:, j * 64 : (j + 1) * 64])
            wsend[half, j] = packed
            target = dev(h=aq, x=m, m=x, y=ye if j else y)
            away = None if j else (x != m) | (rel != 0)
            send(wsend.at[half, j], win.at[rel, j], FIN + 2 * rel + j, target, away)
            if j == 0:

                @pl.when(jnp.logical_not(away))
                def _():
                    win[0, 0] = packed

    for c in ys[0]:
        c.wait_recv()
    for dx in range(4):
        gacc[0, dx] = tile(0, (x + dx) % 4, 0)
    turned[0].wait_recv()
    for dx in range(4):
        gacc[1, dx] = tile(0, (x + dx) % 4, 1)
    for c in ys[1]:
        c.wait_recv()
    first_half = scatter(0)
    turn_far(1)
    turned[1].wait_recv()
    second_half = scatter(1)
    deliver(0, *first_half)
    deliver(1, *second_half)

    for rel in range(2):
        for j in range(2):
            number = FIN + 2 * rel + j
            c = pltpu.make_async_remote_copy(
                src_ref=wsend.at[rel, j], dst_ref=win.at[rel, j],
                send_sem=ssem.at[number], recv_sem=rsem.at[number],
                device_id=dev(x=m, m=x, h=(h + rel) % 2, y=ye if j else y), device_id_type=MESH,
            )
            if rel or j:
                c.wait_recv()
            else:
                pl.when(x != m)(c.wait_recv)
    blocks = []
    for j in range(2):
        w = (win[0, j] + win[1, j]) * (1.0 / 64.0)
        blocks.append(jnp.concatenate([w[:, 0:64], w[:, 64:128]], axis=0))
    first = jnp.where(y // 2 == k, y % 2, 1 - y % 2)
    o_ref[...] = jnp.where(
        first == 0,
        jnp.concatenate(blocks, axis=1),
        jnp.concatenate(blocks[::-1], axis=1),
    )
    for c, when in sends:
        if when is None:
            c.wait_send()
        else:
            pl.when(when)(c.wait_send)


def local(fields, factor):
    f32 = jnp.float32
    hbm = pl.BlockSpec(memory_space=pltpu.HBM)
    return pl.pallas_call(
        kernel,
        out_shape=jax.ShapeDtypeStruct((64, 128), f32),
        in_specs=[hbm, hbm],
        out_specs=pl.BlockSpec(memory_space=pltpu.VMEM),
        scratch_shapes=[
            pltpu.VMEM((2, 4, 2, 64, 256), f32),
            pltpu.VMEM((272, 128), f32),
            pltpu.VMEM((256, 128), f32),
            pltpu.VMEM((2, 4, 2, 64, 128), f32),
            pltpu.VMEM((2, 3, 2, 64, 128), f32),
            pltpu.VMEM((2, 2, 64, 128), f32),
            pltpu.VMEM((2, 64, 128), f32),
            pltpu.VMEM((2, 2, 2, 8, 128), f32),
            pltpu.VMEM((2, 2, 4, 64, 128), f32),
            pltpu.VMEM((2, 2, 2, 64, 128), f32),
            pltpu.VMEM((2, 4, 128, 128), f32),
            pltpu.VMEM((2, 7, 64, 128), f32),
            pltpu.VMEM((2, 7, 64, 128), f32),
            pltpu.VMEM((2, 2, 32, 128), f32),
            pltpu.VMEM((2, 2, 32, 128), f32),
            pltpu.SemaphoreType.DMA((11,)),
            pltpu.SemaphoreType.DMA((COPIES,)),
            pltpu.SemaphoreType.DMA((COPIES,)),
            pltpu.SemaphoreType.REGULAR,
        ],
        compiler_params=pltpu.CompilerParams(
            collective_id=0, has_side_effects=True, vmem_limit_bytes=60 << 20
        ),
        cost_estimate=pl.CostEstimate(flops=135_000_000, bytes_accessed=1_300_000, transcendentals=0),
    )(fields, factor)


def solution(mesh):
    in_specs = (P(None, "gz", "gy", "gx"), P())
    out_specs = P("gy", ("gx", "gz"))
    return jax.shard_map(local, mesh=mesh, in_specs=in_specs, out_specs=out_specs, check_vma=False)
```
